32 devices in a mesh: gr: 4 (over y, core), gc: 8 (over z, x).
Axes of the slice: x: 2, y: 2, z: 4, core: 2. Of those that a mesh axis runs over, the one named last changes fastest.
Arguments:
- features: bfloat16 [4096, 1024], P(('gr', 'gc')), may hold values from -6 to 6
- weight: bfloat16 [1024, 1024], replicated, may hold values from -0.1875 to 0.1875
- cotangent: bfloat16 [4096, 1024], P(('gr', 'gc')), may hold values from -6 to 6
- block_values: bfloat16 [32, 4, 128, 128], P(('gr', 'gc')), as said below
- block_codes: int32 [32, 4], P(('gr', 'gc')), may hold values from 0 to 31, as said below
- block_count: int32 [32], P(('gr', 'gc')), may hold values from 1 to 4, as said below
Outputs:
- output: float32 [4096, 1024], P(('gr', 'gc'))
- input_grad: float32 [4096, 1024], P(('gr', 'gc'))
- weight_grad: float32 [1024, 1024], P('gc')
The draws below stay inside these ranges and needn't reach their ends.
Inputs may be any that keep to these rules, and one draw needn't show every extreme that they name: `block_codes`: write code = row * 32 + column. In every slot, row lies in 0 to 0 and column is a block of a slice s + j * 8 with |j| <= 2 (same grid column, at most 2 grid rows away). The codes of the live slots of one slice differ from one another. Every diagonal block (block row equal to block column) is live. The live slots of a slice are its first block_count slots; the entries of later slots are not part of the adjacency. In every draw some slice has all 4 slots live. `block_values`: the adjacency is symmetric: a block is live exactly when its mirror block is, and its entries are the transpose of the mirror's.
All inputs are finite; a program needn't handle non-finite values.
Results may differ from the reference program's by a relative error of at most 0.0045.
Values may be sent and summed in bfloat16 or wider, within the bound.
A program may use at most 64 MiB of HBM per device.

```python
import jax
import jax.numpy as jnp
from jax import lax

F = 1024
BLK = 128
ROWS = 128
REACH = 2
ROWBLK = 1
MAXB = 4
SLICES = 32
NODES = 4096
NB = 32
N_GR = 4
N_GC = 8


def block_layout(key):
    slot_ids = jnp.arange(MAXB)
    row_in = slot_ids // (N_GR * ROWBLK)
    target_row = slot_ids // ROWBLK % N_GR
    col_in = slot_ids % ROWBLK
    slice_ids = jnp.arange(SLICES)[:, None]
    shift_rows = target_row[None, :] - slice_ids // N_GC
    inside = jnp.abs(shift_rows) <= REACH
    src_block = slice_ids * ROWBLK + row_in[None, :]
    dst_block = (slice_ids + shift_rows * N_GC) * ROWBLK + col_in[None, :]
    dst_block = jnp.where(inside, dst_block, src_block)
    low_block = jnp.minimum(src_block, dst_block)
    high_block = jnp.maximum(src_block, dst_block)
    pair_span = REACH * N_GC * ROWBLK + ROWBLK
    pair_ids = low_block * pair_span + (high_block - low_block)
    pair_draw = jax.random.randint(jax.random.fold_in(key, 11), (NB * pair_span,), 0, 100)
    chosen = pair_draw[pair_ids] < 60
    full_slice = REACH * N_GC
    touches = (slice_ids == full_slice) | (dst_block // ROWBLK == full_slice)
    active = inside & (chosen | (src_block == dst_block) | touches)
    slot_order = jnp.argsort(1 - active.astype(jnp.int32), axis=1, stable=True)
    codes = row_in[None, :] * NB + dst_block
    slot_codes = jnp.take_along_axis(codes, slot_order, axis=1).astype(jnp.int32)
    ordered_pairs = jnp.take_along_axis(pair_ids, slot_order, axis=1)
    flipped = jnp.take_along_axis(src_block > dst_block, slot_order, axis=1)
    diagonal = jnp.take_along_axis(src_block == dst_block, slot_order, axis=1)
    block_total = jnp.sum(active.astype(jnp.int32), axis=1).astype(jnp.int32)
    return (slot_codes, block_total, ordered_pairs, flipped, diagonal)


def draw_block_values(key, part):
    slot_codes, block_total, ordered_pairs, flipped, diagonal = block_layout(key)
    spread = (BLK * ROWBLK * (2 * REACH + 1) * 0.6) ** (-0.5)
    value_key = jax.random.fold_in(key, 23)

    def one_block(pair_id):
        sub_key = jax.random.fold_in(value_key, pair_id)
        return jax.random.normal(sub_key, (BLK, BLK), jnp.float32)
    base = jax.vmap(one_block)(ordered_pairs.reshape(-1)).reshape(SLICES, MAXB, BLK, BLK)
    turned = jnp.swapaxes(base, 2, 3)
    blocks = jnp.where(flipped[:, :, None, None], turned, base)
    blocks = jnp.where(diagonal[:, :, None, None], (base + turned) * 0.7071, blocks)
    return (blocks * spread).astype(jnp.bfloat16)


def draw_block_codes(key, part):
    return block_layout(key)[0]


def draw_block_count(key, part):
    return block_layout(key)[1]


def shard_levels(rng, dims, split, smallest, top_value):
    def one(dim, blocks):
        draws = jax.random.uniform(jax.random.fold_in(jax.random.fold_in(rng, 6), dim), (blocks,), jnp.float32, smallest / len(split), top_value / len(split))
        return jnp.repeat(jnp.exp(draws), dims[dim] // blocks).reshape((-1,) + (1,) * (len(dims) - dim - 1))

    loudness = one(*split[0])
    for cut in split[1:]:
        loudness = loudness * one(*cut)
    return loudness


def centred(own_key, shape, deviation, limit, pieces=(), dtype=jnp.bfloat16):
    values = jax.random.normal(own_key, shape, jnp.float32) * deviation
    if len(pieces) > 0:
        values = shard_levels(own_key, shape, pieces, -0.22, 0.18) * values
    return jnp.clip(values, min=-limit, max=limit).astype(dtype)


def setup_inputs(seed: int = 0) -> dict:
    streams_of = jax.random.split(jax.random.key(seed), 7)
    features = centred(streams_of[0], (NODES, F), 1.0, 6.0, ((0, 32),))
    weight = centred(streams_of[1], (F, F), F ** -0.5, 0.1875)
    cotangent = centred(streams_of[2], (NODES, F), 1.0, 6.0, ((0, 32),))
    block_values = draw_block_values(jax.random.fold_in(streams_of[6], 71), 0)
    block_codes = draw_block_codes(jax.random.fold_in(streams_of[6], 71), 0)
    block_count = draw_block_count(jax.random.fold_in(streams_of[6], 71), 0)
    return {"features": features, "weight": weight, "cotangent": cotangent, "block_values": block_values, "block_codes": block_codes, "block_count": block_count}


def reference(features, weight, cotangent, block_values, block_codes, block_count):
    projected = jnp.dot(features, weight, preferred_element_type=jnp.float32).astype(jnp.bfloat16)
    proj_blocks = projected.reshape(NB, BLK, F)
    slot_ids = jnp.arange(MAXB)
    row_choices = jnp.arange(ROWBLK)

    def forward_slice(slice_item):
        values, slot_codes, block_total = slice_item
        active = slot_ids < block_total
        row_index = slot_codes // NB
        column_block = slot_codes % NB
        gathered_rows = proj_blocks[column_block].astype(jnp.float32)
        products = jnp.einsum("kij,kjf->kif", values.astype(jnp.float32), gathered_rows)
        select_row = ((row_index[:, None] == row_choices[None, :]) & active[:, None]).astype(jnp.float32)
        return jnp.einsum("ka,kif->aif", select_row, products).reshape(ROWS, F)

    summed = lax.map(forward_slice, (block_values, block_codes, block_count)).reshape(NODES, F)
    sigmoid = jax.nn.sigmoid(summed)
    output = summed * sigmoid
    act_slope = (cotangent.astype(jnp.float32) * sigmoid * (1.0 + summed * (1.0 - sigmoid))).astype(jnp.bfloat16)
    slope_blocks = act_slope.reshape(SLICES, ROWBLK, BLK, F)

    def backward_slice(running, slice_item):
        values, slot_codes, block_total, slope_here = slice_item
        active = (slot_ids < block_total).astype(jnp.float32)
        row_index = slot_codes // NB
        column_block = slot_codes % NB
        source_rows = slope_here[row_index].astype(jnp.float32)
        products = jnp.einsum("kij,kif->kjf", values.astype(jnp.float32), source_rows) * active[:, None, None]
        return running.at[column_block].add(products), None

    grad_blocks, unused = lax.scan(backward_slice, jnp.zeros((NB, BLK, F), jnp.float32), (block_values, block_codes, block_count, slope_blocks))
    back_grad = grad_blocks.reshape(NODES, F).astype(jnp.bfloat16)
    input_grad = jnp.dot(back_grad, weight.T, preferred_element_type=jnp.float32)
    weight_grad = jnp.dot(features.T, back_grad, preferred_element_type=jnp.float32) * (NODES ** -0.5)
    return output, input_grad, weight_grad
```

```python
import functools

import jax
import jax.numpy as jnp
from jax import lax
from jax.experimental import pallas as pl
from jax.experimental.pallas import tpu as pltpu
from jax.sharding import PartitionSpec as P

MESH = pl.DeviceIdType.MESH


def dense_tile(row_index, block_index, active, values, piece_blocks, row_blocks):
    block_size = values.shape[-1]
    select_col = (block_index[:, None] == jnp.arange(piece_blocks)[None, :]) & active[:, None]
    select_row = row_index[:, None] == jnp.arange(row_blocks)[None, :]
    tiled = jnp.einsum(
        "ka,km,kij->aimj",
        select_row.astype(jnp.bfloat16),
        select_col.astype(jnp.bfloat16),
        values,
        preferred_element_type=jnp.float32,
    )
    return tiled.astype(jnp.bfloat16).reshape(row_blocks * block_size, piece_blocks * block_size)


def aggregate(source, layout):
    row_index, block_index, active, values = layout
    node_rows = source.shape[0]
    block_size = values.shape[-1]
    row_blocks = node_rows // block_size
    portion = lax.all_gather(source, "gr", axis=0, tiled=True)
    tile = dense_tile(
        row_index, block_index, active, values, portion.shape[0] // block_size, row_blocks
    )
    return jnp.dot(tile, portion, preferred_element_type=jnp.float32)


def by_rows(features, weight, cotangent, block_values, block_codes, block_count):
    node_rows = features.shape[0]
    block_size = block_values.shape[-1]
    row_blocks = node_rows // block_size
    grid_cols = lax.axis_size("gc")
    grid_rows = lax.axis_size("gr")
    all_blocks = row_blocks * grid_rows * grid_cols
    slot_codes = block_codes[0]
    row_index = slot_codes // all_blocks
    column_block = slot_codes % all_blocks
    block_index = column_block // row_blocks // grid_cols * row_blocks + column_block % row_blocks
    active = jnp.arange(slot_codes.shape[0]) < block_count[0]
    layout = (row_index, block_index, active, block_values[0])
    projected = jnp.dot(features, weight, preferred_element_type=jnp.float32).astype(jnp.bfloat16)
    summed = aggregate(projected, layout)
    sigmoid = jax.nn.sigmoid(summed)
    output = summed * sigmoid
    act_slope = (cotangent.astype(jnp.float32) * sigmoid * (1.0 + summed * (1.0 - sigmoid))).astype(
        jnp.bfloat16
    )
    back_grad = aggregate(act_slope, layout).astype(jnp.bfloat16)
    input_grad = lax.dot_general(
        back_grad, weight, (((1,), (1,)), ((), ())), preferred_element_type=jnp.float32
    )
    grad_scale = (node_rows * grid_rows * grid_cols) ** (-0.5)
    partial_grad = (
        lax.dot_general(
            features, back_grad, (((0,), (0,)), ((), ())), preferred_element_type=jnp.float32
        )
        * grad_scale
    )
    row_share = lax.psum_scatter(partial_grad, "gc", scatter_dimension=0, tiled=True)
    weight_grad = lax.psum(row_share, "gr")
    return (output, input_grad, weight_grad)


def layer_kernel(
    n_gr, n_gc, scale,
    feat, wt, cot, vals, codes, count,
    out_o, ig_o, wg_o,
    fa, ft, wq, wv, vv, aa, pj, cq, ob, bq, br, iv, xs, xr, ac, zs, zr, wb,
    loc, f_s, f_r, g_s, g_r, a_s, a_r, b_s, b_r, c_s, c_r, o_s, o_r, k_s, k_r,
    x_s, x_r, z_s, z_r, w_s, w_r,
):
    rows, width = feat.shape
    share = width // n_gr
    chips, n_z = n_gr // 2, n_gc // 2
    r, g = lax.axis_index("gr"), lax.axis_index("gc")
    chip, core = r // 2, r % 2
    z, x = g // 2, g % 2
    mate = chip * 2 + 1 - core
    f32, bf16 = jnp.float32, jnp.bfloat16

    def rowsof(s):
        return pl.ds(pl.multiple_of(s * rows, rows), rows)

    def cols(s):
        return pl.ds(pl.multiple_of(s * share, share), share)

    def send(src, dst, ss, rs, where):
        copy = pltpu.make_async_remote_copy(
            src_ref=src, dst_ref=dst, send_sem=ss, recv_sem=rs, device_id=where,
            device_id_type=MESH,
        )
        copy.start()
        return copy

    def peer(j):
        return lax.rem(r + j, n_gr)

    local_w = pltpu.make_async_copy(wt.at[:, cols(r)], wq, loc.at[0])
    local_f = pltpu.make_async_copy(feat, fa.at[r], loc.at[1])
    local_v = pltpu.make_async_copy(vals.at[0], vv, loc.at[2])
    local_c = pltpu.make_async_copy(cot.at[:, cols(r)], cq.at[r], loc.at[3])
    local_all = pltpu.make_async_copy(wt, wv, loc.at[4])
    for copy in (local_v, local_f, local_w, local_c, local_all):
        copy.start()

    barrier = pltpu.get_barrier_semaphore()
    for j in range(1, n_gr):
        pl.semaphore_signal(barrier, inc=1, device_id={"gr": peer(j)}, device_id_type=MESH)
    pl.semaphore_signal(barrier, inc=1, device_id={"gc": z * 2 + 1 - x}, device_id_type=MESH)
    for k in range(1, n_z):
        pl.semaphore_signal(
            barrier, inc=1, device_id={"gc": lax.rem(z + k, n_z) * 2 + x}, device_id_type=MESH
        )
    pl.semaphore_wait(barrier, n_gr - 1 + n_z)

    sent = []
    f_far = [
        send(feat, fa.at[r], f_s.at[d], f_r.at[d], {"gr": lax.rem(chip + d, chips) * 2 + core})
        for d in range(1, chips)
    ]
    f_mate = send(feat, fa.at[r], f_s.at[0], f_r.at[0], {"gr": mate})

    local_v.wait()
    for m in range(n_gr):
        tile = jnp.zeros((rows, rows), f32)
        for k in range(vv.shape[0]):
            hit = jnp.logical_and(k < count[0], (codes[0, k] % (n_gr * n_gc)) // n_gc == m)
            tile = tile + vv[k].astype(f32) * jnp.where(hit, 1.0, 0.0)
        aa[rowsof(r), m * rows:(m + 1) * rows] = tile.astype(bf16)
    a_far = [
        send(aa.at[rowsof(r)], aa.at[rowsof(r)], a_s.at[d], a_r.at[d],
             {"gr": lax.rem(chip + d, chips) * 2 + core})
        for d in range(1, chips)
    ]
    a_mate = send(aa.at[rowsof(r)], aa.at[rowsof(r)], a_s.at[0], a_r.at[0], {"gr": mate})

    def project(s):
        block = fa[s]
        pj[rowsof(s), :] = jnp.dot(block, wq[...], preferred_element_type=f32).astype(bf16)
        ft[:, rowsof(s)] = block.T

    local_f.wait()
    local_w.wait()
    project(r)
    f_mate.wait_recv()
    project(mate)
    f_next = []
    for d in range(1, chips):
        s = lax.rem(chip + chips - d, chips) * 2 + core
        f_far[d - 1].wait_recv()
        f_next.append(send(fa.at[s], fa.at[s], g_s.at[d], g_r.at[d], {"gr": mate}))
    a_next = []
    c_all = [
        send(cot.at[:, cols(peer(j))], cq.at[r], c_s.at[j], c_r.at[j], {"gr": peer(j)})
        for j in range(1, n_gr)
    ]
    for d in range(1, chips):
        project(lax.rem(chip + chips - d, chips) * 2 + core)
    for d in range(1, chips):
        s = lax.rem(chip + chips - d, chips) * 2 + core
        a_far[d - 1].wait_recv()
        a_next.append(send(aa.at[rowsof(s)], aa.at[rowsof(s)], b_s.at[d], b_r.at[d], {"gr": mate}))
    for d in range(1, chips):
        f_next[d - 1].wait_recv()
        project(lax.rem(chip + chips - d, chips) * 2 + 1 - core)
    a_mate.wait_recv()
    for copy in a_next:
        copy.wait_recv()
    local_c.wait()
    for copy in c_all:
        copy.wait_recv()

    for i in range(n_gr):
        summed = jnp.dot(aa[i * rows:(i + 1) * rows, :], pj[...], preferred_element_type=f32)
        sigmoid = jax.nn.sigmoid(summed)
        ob[i] = (summed * sigmoid).astype(bf16)
        slope = cq[i].astype(f32) * sigmoid * (1.0 + summed * (1.0 - sigmoid))
        cq[i] = slope.astype(bf16)
    slope_all = cq[...].reshape(n_gr * rows, share)
    for i in range(n_gr):
        bq[i] = jnp.dot(
            aa[i * rows:(i + 1) * rows, :], slope_all, preferred_element_type=f32
        ).astype(bf16)
    back = bq[...].reshape(n_gr * rows, share)

    depth = width // n_gc

    def grad_rows(zz, xx):
        at = pl.ds(pl.multiple_of((zz * 2 + xx) * depth, depth), depth)
        return jnp.dot(ft[at, :], back, preferred_element_type=f32)

    order = [k % n_z for k in range(1, n_z + 1)]
    x_all = {}
    for k in order:
        xs[k] = grad_rows(lax.rem(z + k, n_z), 1 - x).astype(bf16)
        x_all[k] = send(xs.at[k], xr.at[k], x_s.at[k], x_r.at[k], {"gc": z * 2 + 1 - x})
    k_all = [
        send(bq.at[peer(j)], br.at[:, cols(r)], k_s.at[j], k_r.at[j], {"gr": peer(j)})
        for j in range(1, n_gr)
    ]
    o_all = [
        send(ob.at[peer(j)], out_o.at[:, cols(r)], o_s.at[j], o_r.at[j], {"gr": peer(j)})
        for j in range(1, n_gr)
    ]
    own_o = pltpu.make_async_copy(ob.at[r], out_o.at[:, cols(r)], loc.at[5])
    own_o.start()
    br[:, cols(r)] = bq[r]
    for k in order:
        ac[k] = grad_rows(lax.rem(z + k, n_z), x)
    z_all = {}
    for k in order:
        x_all[k].wait_recv()
        if k > 0:
            zs[k] = (ac[k] + xr[k].astype(f32)).astype(bf16)
            z_all[k] = send(
                zs.at[k], zr.at[k], z_s.at[k], z_r.at[k], {"gc": lax.rem(z + k, n_z) * 2 + x}
            )
    for copy in k_all:
        copy.wait_recv()
    local_all.wait()
    step = 256
    for i in range(width // step):
        iv[:, i * step:(i + 1) * step] = lax.dot_general(
            br[...], wv[i * step:(i + 1) * step, :], (((1,), (1,)), ((), ())),
            preferred_element_type=f32,
        )
    own_i = pltpu.make_async_copy(iv, ig_o, loc.at[6])
    own_i.start()
    total = ac[0] + xr[0].astype(f32)
    for k in range(1, n_z):
        z_all[k].wait_recv()
        total = total + zr[k].astype(f32)
    wb[...] = (total * scale).astype(bf16)
    w_all = [
        send(wb, wg_o.at[:, cols(r)], w_s.at[j], w_r.at[j], {"gr": peer(j)})
        for j in range(1, n_gr)
    ]
    own_w = pltpu.make_async_copy(wb, wg_o.at[:, cols(r)], loc.at[7])
    own_w.start()
    for copy in [f_mate, a_mate] + f_far + a_far + f_next + a_next + c_all:
        copy.wait_send()
    for copy in list(x_all.values()) + list(z_all.values()) + k_all:
        copy.wait_send()
    for copy in o_all + w_all:
        copy.wait()
    own_o.wait()
    own_i.wait()
    own_w.wait()


def by_columns(features, weight, cotangent, block_values, block_codes, block_count):
    n_gr, n_gc = lax.axis_size("gr"), lax.axis_size("gc")
    rows, width = features.shape
    slots = block_values.shape[1]
    share, depth, n_z = width // n_gr, width // n_gc, n_gc // 2
    f32, bf16 = jnp.float32, jnp.bfloat16
    dma = pltpu.SemaphoreType.DMA
    everywhere = pl.BlockSpec(memory_space=pl.ANY)
    scalars = pl.BlockSpec(memory_space=pltpu.SMEM)
    chips = n_gr // 2
    out, input_grad, weight_grad = pl.pallas_call(
        functools.partial(layer_kernel, n_gr, n_gc, (rows * n_gr * n_gc) ** (-0.5)),
        out_shape=(
            jax.ShapeDtypeStruct((rows, width), bf16),
            jax.ShapeDtypeStruct((rows, width), f32),
            jax.ShapeDtypeStruct((depth, width), bf16),
        ),
        in_specs=[everywhere] * 4 + [scalars] * 2,
        out_specs=(everywhere,) * 3,
        scratch_shapes=[
            pltpu.VMEM((n_gr, rows, width), bf16),
            pltpu.VMEM((width, n_gr * rows), bf16),
            pltpu.VMEM((width, share), bf16),
            pltpu.VMEM((width, width), bf16),
            pltpu.VMEM((slots, rows, rows), bf16),
            pltpu.VMEM((n_gr * rows, n_gr * rows), bf16),
            pltpu.VMEM((n_gr * rows, share), bf16),
            pltpu.VMEM((n_gr, rows, share), bf16),
            pltpu.VMEM((n_gr, rows, share), bf16),
            pltpu.VMEM((n_gr, rows, share), bf16),
            pltpu.VMEM((rows, width), bf16),
            pltpu.VMEM((rows, width), f32),
            pltpu.VMEM((n_z, depth, share), bf16),
            pltpu.VMEM((n_z, depth, share), bf16),
            pltpu.VMEM((n_z, depth, share), f32),
            pltpu.VMEM((n_z, depth, share), bf16),
            pltpu.VMEM((n_z, depth, share), bf16),
            pltpu.VMEM((depth, share), bf16),
            dma((8,)),
        ]
        + [dma((chips,))] * 8
        + [dma((n_gr,))] * 6
        + [dma((n_z,))] * 4
        + [dma((n_gr,))] * 2,
        compiler_params=pltpu.CompilerParams(
            collective_id=0, has_side_effects=True, vmem_limit_bytes=32 * 1024 * 1024
        ),
        cost_estimate=pl.CostEstimate(
            flops=2 * rows * width * (3 * width + 2 * n_gr * rows),
            bytes_accessed=6 * width * width,
            transcendentals=rows * width,
        ),
    )(features, weight, cotangent, block_values, block_codes, block_count)
    return (out.astype(f32), input_grad, weight_grad.astype(f32))


def local(features, weight, cotangent, block_values, block_codes, block_count):
    n_gr, n_gc = lax.axis_size("gr"), lax.axis_size("gc")
    rows, width = features.shape
    whole = width % (128 * n_gr) == 0 and width % (16 * n_gc) == 0
    even = n_gr % 2 == 0 and n_gc % 2 == 0
    take = by_columns if whole and even and rows == block_values.shape[-1] else by_rows
    return take(features, weight, cotangent, block_values, block_codes, block_count)


def solution(mesh):
    in_specs = (
        P(("gr", "gc"), None),
        P(),
        P(("gr", "gc"), None),
        P(("gr", "gc"), None, None, None),
        P(("gr", "gc"), None),
        P(("gr", "gc")),
    )
    out_specs = (P(("gr", "gc"), None), P(("gr", "gc"), None), P("gc", None))
    return jax.shard_map(local, mesh=mesh, in_specs=in_specs, out_specs=out_specs, check_vma=False)
```

```python
import functools

import jax
import jax.numpy as jnp
from jax import lax
from jax.experimental import pallas as pl
from jax.experimental.pallas import tpu as pltpu
from jax.sharding import PartitionSpec as P

MESH = pl.DeviceIdType.MESH
GRANT = 62 * 1024 * 1024


def dense_tile(row_index, block_index, active, values, piece_blocks, row_blocks):
    block_size = values.shape[-1]
    select_col = (block_index[:, None] == jnp.arange(piece_blocks)[None, :]) & active[:, None]
    select_row = row_index[:, None] == jnp.arange(row_blocks)[None, :]
    tiled = jnp.einsum(
        "ka,km,kij->aimj",
        select_row.astype(jnp.bfloat16),
        select_col.astype(jnp.bfloat16),
        values,
        preferred_element_type=jnp.float32,
    )
    return tiled.astype(jnp.bfloat16).reshape(row_blocks * block_size, piece_blocks * block_size)


def aggregate(source, layout):
    row_index, block_index, active, values = layout
    node_rows = source.shape[0]
    block_size = values.shape[-1]
    row_blocks = node_rows // block_size
    portion = lax.all_gather(source, "gr", axis=0, tiled=True)
    tile = dense_tile(
        row_index, block_index, active, values, portion.shape[0] // block_size, row_blocks
    )
    return jnp.dot(tile, portion, preferred_element_type=jnp.float32)


def by_rows(features, weight, cotangent, block_values, block_codes, block_count):
    node_rows = features.shape[0]
    block_size = block_values.shape[-1]
    row_blocks = node_rows // block_size
    grid_cols = lax.axis_size("gc")
    grid_rows = lax.axis_size("gr")
    all_blocks = row_blocks * grid_rows * grid_cols
    slot_codes = block_codes[0]
    row_index = slot_codes // all_blocks
    column_block = slot_codes % all_blocks
    block_index = column_block // row_blocks // grid_cols * row_blocks + column_block % row_blocks
    active = jnp.arange(slot_codes.shape[0]) < block_count[0]
    layout = (row_index, block_index, active, block_values[0])
    projected = jnp.dot(features, weight, preferred_element_type=jnp.float32).astype(jnp.bfloat16)
    summed = aggregate(projected, layout)
    sigmoid = jax.nn.sigmoid(summed)
    output = summed * sigmoid
    act_slope = (cotangent.astype(jnp.float32) * sigmoid * (1.0 + summed * (1.0 - sigmoid))).astype(
        jnp.bfloat16
    )
    back_grad = aggregate(act_slope, layout).astype(jnp.bfloat16)
    input_grad = lax.dot_general(
        back_grad, weight, (((1,), (1,)), ((), ())), preferred_element_type=jnp.float32
    )
    grad_scale = (node_rows * grid_rows * grid_cols) ** (-0.5)
    partial_grad = (
        lax.dot_general(
            features, back_grad, (((0,), (0,)), ((), ())), preferred_element_type=jnp.float32
        )
        * grad_scale
    )
    row_share = lax.psum_scatter(partial_grad, "gc", scatter_dimension=0, tiled=True)
    weight_grad = lax.psum(row_share, "gr")
    return (output, input_grad, weight_grad)


def layer_kernel(
    n_gr, n_gc, scale,
    feat, wt, cot, vals, codes, count,
    out_o, ig_o, wg_o,
    fa, ft, wq, wv, vv, aa, pj, cq, sl, ob, bq, br, iv, xs, xr, ac, zs, zr, wa,
    loc, f_s, f_r, g_s, g_r, a_s, a_r, b_s, b_r, w_s, w_r, v_s, v_r,
    c_s, c_r, o_s, o_r, k_s, k_r, x_s, x_r, z_s, z_r,
):
    rows, width = feat.shape
    share = width // n_gr
    chips, n_z = n_gr // 2, n_gc // 2
    r, g = lax.axis_index("gr"), lax.axis_index("gc")
    chip, core = r // 2, r % 2
    z, x = g // 2, g % 2
    mate = chip * 2 + 1 - core
    f32, bf16 = jnp.float32, jnp.bfloat16

    def rowsof(s):
        return pl.ds(pl.multiple_of(s * rows, rows), rows)

    def cols(s):
        return pl.ds(pl.multiple_of(s * share, share), share)

    def flip(at, m):
        for bit in (1 << b for b in range(n_z.bit_length())):
            if m & bit:
                at = at + bit - 2 * bit * (at // bit % 2)
        return at

    def send(src, dst, ss, rs, where):
        copy = pltpu.make_async_remote_copy(
            src_ref=src, dst_ref=dst, send_sem=ss, recv_sem=rs, device_id=where,
            device_id_type=MESH,
        )
        copy.start()
        return copy

    def peer(j):
        return lax.rem(r + j, n_gr)

    local_w = pltpu.make_async_copy(wt.at[:, cols(r)], wq, loc.at[0])
    local_f = pltpu.make_async_copy(feat, fa.at[r], loc.at[1])
    local_v = pltpu.make_async_copy(vals.at[0], vv, loc.at[2])
    local_c = pltpu.make_async_copy(cot.at[:, cols(r)], cq.at[r], loc.at[3])
    local_all = pltpu.make_async_copy(wt, wv, loc.at[4])
    for copy in (local_v, local_f, local_w, local_c, local_all):
        copy.start()

    barrier = pltpu.get_barrier_semaphore()
    for j in range(1, n_gr):
        pl.semaphore_signal(barrier, inc=1, device_id={"gr": peer(j)}, device_id_type=MESH)
    pl.semaphore_signal(barrier, inc=1, device_id={"gc": z * 2 + 1 - x}, device_id_type=MESH)
    bits = [1 << b for b in range(n_z.bit_length() - 1)]
    for bit in bits:
        pl.semaphore_signal(
            barrier, inc=1, device_id={"gc": flip(z, bit) * 2 + x}, device_id_type=MESH
        )
    pl.semaphore_wait(barrier, n_gr + len(bits))

    far = range(1, chips)
    half = rows // 2
    halves = (pl.ds(0, half), pl.ds(half, half))

    def ahead(d):
        return lax.rem(chip + d, chips) * 2 + core

    def behind(d):
        return lax.rem(chip + chips - d, chips) * 2 + core

    f_far = {
        (d, h): send(
            feat.at[part, :], fa.at[r, part, :], f_s.at[d, h], f_r.at[d, h], {"gr": ahead(d)}
        )
        for h, part in enumerate(halves)
        for d in far
    }
    f_mate = send(feat, fa.at[r], f_s.at[0, 0], f_r.at[0, 0], {"gr": mate})

    local_v.wait()
    for m in range(n_gr):
        tile = jnp.zeros((rows, rows), f32)
        for k in range(vv.shape[0]):
            hit = jnp.logical_and(k < count[0], (codes[0, k] % (n_gr * n_gc)) // n_gc == m)
            tile = tile + vv[k].astype(f32) * jnp.where(hit, 1.0, 0.0)
        aa[rowsof(r), m * rows:(m + 1) * rows] = tile.astype(bf16)

    def listed(s):
        if chips == 2:
            pair = pl.ds(pl.multiple_of(s // 2 * (2 * rows), 2 * rows), 2 * rows)
            return aa.at[rowsof(s), pair]
        return aa.at[rowsof(s), :]

    a_far = [send(listed(r), listed(r), a_s.at[d], a_r.at[d], {"gr": ahead(d)}) for d in far]
    a_mate = send(aa.at[rowsof(r)], aa.at[rowsof(r)], a_s.at[0], a_r.at[0], {"gr": mate})

    def project(s):
        block = fa[s]
        pj[rowsof(s), :] = jnp.dot(block, wq[...], preferred_element_type=f32).astype(bf16)
        ft[:, rowsof(s)] = block.T

    local_f.wait()
    local_w.wait()
    project(r)
    f_mate.wait_recv()
    project(mate)

    f_next = {}
    c_all = []
    for h, part in enumerate(halves):
        for d in far:
            f_far[d, h].wait_recv()
            here = fa.at[behind(d), part, :]
            f_next[d, h] = send(here, here, g_s.at[d, h], g_r.at[d, h], {"gr": mate})
        if h == 0:
            c_all = [
                send(cot.at[:, cols(peer(j))], cq.at[r], c_s.at[j], c_r.at[j], {"gr": peer(j)})
                for j in range(1, n_gr)
            ]
    for d in far:
        project(behind(d))
    a_next = []
    for d in far:
        a_far[d - 1].wait_recv()
        here = listed(behind(d))
        a_next.append(send(here, here, b_s.at[d], b_r.at[d], {"gr": mate}))
    a_mate.wait_recv()
    if chips == 2:
        for t in (r, mate):
            for s in (lax.rem(chip + 1, 2) * 2, lax.rem(chip + 1, 2) * 2 + 1):
                aa[rowsof(s), rowsof(t)] = aa[rowsof(t), rowsof(s)].T
    for d in far:
        for h in range(2):
            f_next[d, h].wait_recv()
        project(behind(d) + 1 - 2 * core)
    for copy in a_next:
        copy.wait_recv()

    for i in range(n_gr):
        summed = jnp.dot(aa[i * rows:(i + 1) * rows, :], pj[...], preferred_element_type=f32)
        sigmoid = jax.nn.sigmoid(summed)
        ob[i] = (summed * sigmoid).astype(bf16)
        sl[i] = sigmoid * (1.0 + summed * (1.0 - sigmoid))
    local_c.wait()
    for copy in c_all:
        copy.wait_recv()
    slope_all = (cq[...].astype(f32) * sl[...]).astype(bf16).reshape(n_gr * rows, share)
    for i in range(n_gr):
        bq[i] = jnp.dot(
            aa[i * rows:(i + 1) * rows, :], slope_all, preferred_element_type=f32
        ).astype(bf16)
    back = bq[...].reshape(n_gr * rows, share)

    depth = width // n_gc

    def grad_rows(zz, xx):
        at = pl.ds(pl.multiple_of((zz * 2 + xx) * depth, depth), depth)
        return jnp.dot(ft[at, :], back, preferred_element_type=f32)

    order = range(n_z - 1, -1, -1)
    x_all = {}
    for k in order:
        xs[k] = grad_rows(flip(z, k), 1 - x).astype(bf16)
        x_all[k] = send(xs.at[k], xr.at[k], x_s.at[k], x_r.at[k], {"gc": z * 2 + 1 - x})
    k_all = [
        send(bq.at[peer(j)], br.at[:, cols(r)], k_s.at[j], k_r.at[j], {"gr": peer(j)})
        for j in range(1, n_gr)
    ]
    o_all = [
        send(ob.at[peer(j)], out_o.at[:, cols(r)], o_s.at[j], o_r.at[j], {"gr": peer(j)})
        for j in range(1, n_gr)
    ]
    own_o = pltpu.make_async_copy(ob.at[r], out_o.at[:, cols(r)], loc.at[5])
    own_o.start()
    br[:, cols(r)] = bq[r]
    for k in order:
        ac[k] = grad_rows(flip(z, k), x)

    z_all = {}

    def gathered(k):
        x_all[k].wait_recv()
        total = ac[k] + xr[k].astype(f32)
        for bit in bits:
            if k & bit:
                break
            z_all[k + bit].wait_recv()
            total = total + zr[k + bit].astype(f32)
        return total

    for k in order[:-1]:
        zs[k] = gathered(k).astype(bf16)
        low = k & -k
        z_all[k] = send(
            zs.at[k], zr.at[k], z_s.at[k], z_r.at[k], {"gc": flip(z, low) * 2 + x}
        )
    for copy in k_all:
        copy.wait_recv()
    local_all.wait()
    step = 256
    for i in range(width // step):
        iv[:, i * step:(i + 1) * step] = lax.dot_general(
            br[...], wv[i * step:(i + 1) * step, :], (((1,), (1,)), ((), ())),
            preferred_element_type=f32,
        )
    own_i = pltpu.make_async_copy(iv, ig_o, loc.at[6])
    own_i.start()
    wa[r] = (gathered(0) * scale).astype(bf16)
    w_far = [send(wa.at[r], wa.at[r], w_s.at[d], w_r.at[d], {"gr": ahead(d)}) for d in far]
    w_mate = send(wa.at[r], wa.at[r], w_s.at[0], w_r.at[0], {"gr": mate})
    w_out = []

    def keep(s, j):
        w_out.append(pltpu.make_async_copy(wa.at[s], wg_o.at[:, cols(s)], loc.at[7 + j]))
        w_out[-1].start()

    keep(r, 0)
    w_next = []
    for d in far:
        w_far[d - 1].wait_recv()
        s = behind(d)
        w_next.append(send(wa.at[s], wa.at[s], v_s.at[d], v_r.at[d], {"gr": mate}))
        keep(s, 2 * d)
    w_mate.wait_recv()
    keep(mate, 1)
    for d in far:
        w_next[d - 1].wait_recv()
        keep(behind(d) + 1 - 2 * core, 2 * d + 1)
    for copy in [f_mate, a_mate, w_mate] + a_far + a_next + w_far + w_next + c_all + k_all:
        copy.wait_send()
    for group in (f_far, f_next, x_all, z_all):
        for copy in group.values():
            copy.wait_send()
    for copy in o_all:
        copy.wait()
    for copy in w_out:
        copy.wait()
    own_o.wait()
    own_i.wait()


def finish_kernel(out_b, ig, wg_b, out_o, ig_o, wg_o, sem):
    copy = pltpu.make_async_copy(ig, ig_o, sem)
    copy.start()
    out_o[...] = out_b[...].astype(jnp.float32)
    wg_o[...] = wg_b[...].astype(jnp.float32)
    copy.wait()


def by_columns(features, weight, cotangent, block_values, block_codes, block_count):
    n_gr, n_gc = lax.axis_size("gr"), lax.axis_size("gc")
    rows, width = features.shape
    slots = block_values.shape[1]
    share, depth, n_z = width // n_gr, width // n_gc, n_gc // 2
    f32, bf16 = jnp.float32, jnp.bfloat16
    dma = pltpu.SemaphoreType.DMA
    everywhere = pl.BlockSpec(memory_space=pl.ANY)
    outside = pl.BlockSpec(memory_space=pltpu.HBM)
    inside = pl.BlockSpec(memory_space=pltpu.VMEM)
    scalars = pl.BlockSpec(memory_space=pltpu.SMEM)
    chips = n_gr // 2
    out, input_grad, weight_grad = pl.pallas_call(
        functools.partial(layer_kernel, n_gr, n_gc, (rows * n_gr * n_gc) ** (-0.5)),
        out_shape=(
            jax.ShapeDtypeStruct((rows, width), bf16),
            jax.ShapeDtypeStruct((rows, width), f32),
            jax.ShapeDtypeStruct((depth, width), bf16),
        ),
        in_specs=[outside] * 4 + [scalars] * 2,
        out_specs=(everywhere,) * 3,
        scratch_shapes=[
            pltpu.VMEM((n_gr, rows, width), bf16),
            pltpu.VMEM((width, n_gr * rows), bf16),
            pltpu.VMEM((width, share), bf16),
            pltpu.VMEM((width, width), bf16),
            pltpu.VMEM((slots, rows, rows), bf16),
            pltpu.VMEM((n_gr * rows, n_gr * rows), bf16),
            pltpu.VMEM((n_gr * rows, share), bf16),
            pltpu.VMEM((n_gr, rows, share), bf16),
            pltpu.VMEM((n_gr, rows, share), f32),
            pltpu.VMEM((n_gr, rows, share), bf16),
            pltpu.VMEM((n_gr, rows, share), bf16),
            pltpu.VMEM((rows, width), bf16),
            pltpu.VMEM((rows, width), f32),
            pltpu.VMEM((n_z, depth, share), bf16),
            pltpu.VMEM((n_z, depth, share), bf16),
            pltpu.VMEM((n_z, depth, share), f32),
            pltpu.VMEM((n_z, depth, share), bf16),
            pltpu.VMEM((n_z, depth, share), bf16),
            pltpu.VMEM((n_gr, depth, share), bf16),
            dma((7 + n_gr,)),
        ]
        + [dma((chips, 2))] * 4
        + [dma((chips,))] * 8
        + [dma((n_gr,))] * 6
        + [dma((n_z,))] * 4,
        compiler_params=pltpu.CompilerParams(
            collective_id=0, has_side_effects=True, vmem_limit_bytes=GRANT
        ),
        cost_estimate=pl.CostEstimate(
            flops=2 * rows * width * (3 * width + 2 * n_gr * rows),
            bytes_accessed=6 * width * width,
            transcendentals=rows * width,
        ),
    )(features, weight, cotangent, block_values, block_codes, block_count)
    return pl.pallas_call(
        finish_kernel,
        out_shape=(
            jax.ShapeDtypeStruct((rows, width), f32),
            jax.ShapeDtypeStruct((rows, width), f32),
            jax.ShapeDtypeStruct((depth, width), f32),
        ),
        in_specs=[inside, everywhere, inside],
        out_specs=(inside, everywhere, inside),
        scratch_shapes=[dma(())],
        compiler_params=pltpu.CompilerParams(vmem_limit_bytes=GRANT),
    )(out, input_grad, weight_grad)


def local(features, weight, cotangent, block_values, block_codes, block_count):
    n_gr, n_gc = lax.axis_size("gr"), lax.axis_size("gc")
    rows, width = features.shape
    whole = width % (128 * n_gr) == 0 and width % (16 * n_gc) == 0
    even = n_gr % 2 == 0 and n_gc in (2, 4, 8, 16, 32)
    take = by_columns if whole and even and rows == block_values.shape[-1] else by_rows
    return take(features, weight, cotangent, block_values, block_codes, block_count)


def solution(mesh):
    in_specs = (
        P(("gr", "gc"), None),
        P(),
        P(("gr", "gc"), None),
        P(("gr", "gc"), None, None, None),
        P(("gr", "gc"), None),
        P(("gr", "gc")),
    )
    out_specs = (P(("gr", "gc"), None), P(("gr", "gc"), None), P("gc", None))
    return jax.shard_map(local, mesh=mesh, in_specs=in_specs, out_specs=out_specs, check_vma=False)
```

```python
import functools

import jax
import jax.numpy as jnp
from jax import lax
from jax.experimental import pallas as pl
from jax.experimental.pallas import tpu as pltpu
from jax.sharding import PartitionSpec as P

MESH = pl.DeviceIdType.MESH
GRANT = 62 * 1024 * 1024


def dense_tile(row_index, block_index, active, values, piece_blocks, row_blocks):
    block_size = values.shape[-1]
    select_col = (block_index[:, None] == jnp.arange(piece_blocks)[None, :]) & active[:, None]
    select_row = row_index[:, None] == jnp.arange(row_blocks)[None, :]
    tiled = jnp.einsum(
        "ka,km,kij->aimj",
        select_row.astype(jnp.bfloat16),
        select_col.astype(jnp.bfloat16),
        values,
        preferred_element_type=jnp.float32,
    )
    return tiled.astype(jnp.bfloat16).reshape(row_blocks * block_size, piece_blocks * block_size)


def aggregate(source, layout):
    row_index, block_index, active, values = layout
    node_rows = source.shape[0]
    block_size = values.shape[-1]
    row_blocks = node_rows // block_size
    portion = lax.all_gather(source, "gr", axis=0, tiled=True)
    tile = dense_tile(
        row_index, block_index, active, values, portion.shape[0] // block_size, row_blocks
    )
    return jnp.dot(tile, portion, preferred_element_type=jnp.float32)


def by_rows(features, weight, cotangent, block_values, block_codes, block_count):
    node_rows = features.shape[0]
    block_size = block_values.shape[-1]
    row_blocks = node_rows // block_size
    grid_cols = lax.axis_size("gc")
    grid_rows = lax.axis_size("gr")
    all_blocks = row_blocks * grid_rows * grid_cols
    slot_codes = block_codes[0]
    row_index = slot_codes // all_blocks
    column_block = slot_codes % all_blocks
    block_index = column_block // row_blocks // grid_cols * row_blocks + column_block % row_blocks
    active = jnp.arange(slot_codes.shape[0]) < block_count[0]
    layout = (row_index, block_index, active, block_values[0])
    projected = jnp.dot(features, weight, preferred_element_type=jnp.float32).astype(jnp.bfloat16)
    summed = aggregate(projected, layout)
    sigmoid = jax.nn.sigmoid(summed)
    output = summed * sigmoid
    act_slope = (cotangent.astype(jnp.float32) * sigmoid * (1.0 + summed * (1.0 - sigmoid))).astype(
        jnp.bfloat16
    )
    back_grad = aggregate(act_slope, layout).astype(jnp.bfloat16)
    input_grad = lax.dot_general(
        back_grad, weight, (((1,), (1,)), ((), ())), preferred_element_type=jnp.float32
    )
    grad_scale = (node_rows * grid_rows * grid_cols) ** (-0.5)
    partial_grad = (
        lax.dot_general(
            features, back_grad, (((0,), (0,)), ((), ())), preferred_element_type=jnp.float32
        )
        * grad_scale
    )
    row_share = lax.psum_scatter(partial_grad, "gc", scatter_dimension=0, tiled=True)
    weight_grad = lax.psum(row_share, "gr")
    return (output, input_grad, weight_grad)


def layer_kernel(
    n_gr, n_gc, scale,
    feat, wt, cot, vals, codes, count,
    out_o, ig_o, wg_o,
    fa, ft, wq, wv, vv, aa, pj, cq, sl, ob, bq, br, iv, xs, xr, ac, wa,
    loc, f_s, f_r, g_s, g_r, a_s, a_r, b_s, b_r, w_s, w_r, v_s, v_r,
    c_s, c_r, o_s, o_r, k_s, k_r, x_s, x_r,
):
    rows, width = feat.shape
    share = width // n_gr
    chips = n_gr // 2
    r, g = lax.axis_index("gr"), lax.axis_index("gc")
    chip, core = r // 2, r % 2
    mate = chip * 2 + 1 - core
    f32, bf16 = jnp.float32, jnp.bfloat16

    def rowsof(s):
        return pl.ds(pl.multiple_of(s * rows, rows), rows)

    def cols(s):
        return pl.ds(pl.multiple_of(s * share, share), share)

    def flip(at, m):
        for bit in (1 << b for b in range(n_gc.bit_length())):
            if m & bit:
                at = at + bit - 2 * bit * (at // bit % 2)
        return at

    def send(src, dst, ss, rs, where):
        copy = pltpu.make_async_remote_copy(
            src_ref=src, dst_ref=dst, send_sem=ss, recv_sem=rs, device_id=where,
            device_id_type=MESH,
        )
        copy.start()
        return copy

    def peer(j):
        return lax.rem(r + j, n_gr)

    local_w = pltpu.make_async_copy(wt.at[:, cols(r)], wq, loc.at[0])
    local_f = pltpu.make_async_copy(feat, fa.at[r], loc.at[1])
    local_v = pltpu.make_async_copy(vals.at[0], vv, loc.at[2])
    local_c = pltpu.make_async_copy(cot.at[:, cols(r)], cq.at[r], loc.at[3])
    local_all = pltpu.make_async_copy(wt, wv, loc.at[4])
    for copy in (local_v, local_f, local_w, local_c, local_all):
        copy.start()

    barrier = pltpu.get_barrier_semaphore()
    for j in range(1, n_gr):
        pl.semaphore_signal(barrier, inc=1, device_id={"gr": peer(j)}, device_id_type=MESH)
    bits = [1 << b for b in range(n_gc.bit_length() - 1)]
    for bit in bits:
        pl.semaphore_signal(barrier, inc=1, device_id={"gc": flip(g, bit)}, device_id_type=MESH)
    pl.semaphore_wait(barrier, n_gr - 1 + len(bits))

    far = range(1, chips)
    half = rows // 2
    halves = (pl.ds(0, half), pl.ds(half, half))

    def ahead(d):
        return lax.rem(chip + d, chips) * 2 + core

    def behind(d):
        return lax.rem(chip + chips - d, chips) * 2 + core

    f_far = {
        (d, h): send(
            feat.at[part, :], fa.at[r, part, :], f_s.at[d, h], f_r.at[d, h], {"gr": ahead(d)}
        )
        for h, part in enumerate(halves)
        for d in far
    }
    f_mate = send(feat, fa.at[r], f_s.at[0, 0], f_r.at[0, 0], {"gr": mate})

    local_v.wait()
    for m in range(n_gr):
        tile = jnp.zeros((rows, rows), f32)
        for k in range(vv.shape[0]):
            hit = jnp.logical_and(k < count[0], (codes[0, k] % (n_gr * n_gc)) // n_gc == m)
            tile = tile + vv[k].astype(f32) * jnp.where(hit, 1.0, 0.0)
        aa[rowsof(r), m * rows:(m + 1) * rows] = tile.astype(bf16)

    def listed(s):
        if chips == 2:
            pair = pl.ds(pl.multiple_of(s // 2 * (2 * rows), 2 * rows), 2 * rows)
            return aa.at[rowsof(s), pair]
        return aa.at[rowsof(s), :]

    a_far = [send(listed(r), listed(r), a_s.at[d], a_r.at[d], {"gr": ahead(d)}) for d in far]
    a_mate = send(aa.at[rowsof(r)], aa.at[rowsof(r)], a_s.at[0], a_r.at[0], {"gr": mate})

    def project(s):
        pj[rowsof(s), :] = jnp.dot(fa[s], wq[...], preferred_element_type=f32).astype(bf16)

    def turn(s):
        ft[:, rowsof(s)] = fa[s].T

    local_f.wait()
    local_w.wait()
    project(r)
    turn(r)
    f_mate.wait_recv()
    project(mate)
    turn(mate)

    f_next = {}
    c_all = []
    for h, part in enumerate(halves):
        for d in far:
            f_far[d, h].wait_recv()
            here = fa.at[behind(d), part, :]
            f_next[d, h] = send(here, here, g_s.at[d, h], g_r.at[d, h], {"gr": mate})
        if h == 0:
            c_all = [
                send(cot.at[:, cols(peer(j))], cq.at[r], c_s.at[j], c_r.at[j], {"gr": peer(j)})
                for j in range(1, n_gr)
            ]
    a_next = []
    for d in far:
        a_far[d - 1].wait_recv()
        here = listed(behind(d))
        a_next.append(send(here, here, b_s.at[d], b_r.at[d], {"gr": mate}))
    for d in far:
        project(behind(d))
    a_mate.wait_recv()
    if chips == 2:
        for t in (r, mate):
            for s in (lax.rem(chip + 1, 2) * 2, lax.rem(chip + 1, 2) * 2 + 1):
                aa[rowsof(s), rowsof(t)] = aa[rowsof(t), rowsof(s)].T
    for d in far:
        for h in range(2):
            f_next[d, h].wait_recv()
        project(behind(d) + 1 - 2 * core)
    for copy in a_next:
        copy.wait_recv()

    for i in range(n_gr):
        summed = jnp.dot(aa[i * rows:(i + 1) * rows, :], pj[...], preferred_element_type=f32)
        sigmoid = jax.nn.sigmoid(summed)
        ob[i] = (summed * sigmoid).astype(bf16)
        sl[i] = sigmoid * (1.0 + summed * (1.0 - sigmoid))
    for d in far:
        turn(behind(d))
        turn(behind(d) + 1 - 2 * core)
    local_c.wait()
    for copy in c_all:
        copy.wait_recv()
    slope_all = (cq[...].astype(f32) * sl[...]).astype(bf16).reshape(n_gr * rows, share)
    for i in range(n_gr):
        bq[i] = jnp.dot(
            aa[i * rows:(i + 1) * rows, :], slope_all, preferred_element_type=f32
        ).astype(bf16)
    back = bq[...].reshape(n_gr * rows, share)

    depth, part = width // n_gc, share // 2
    sides = [bits, bits[1::-1] + bits[2:]]
    x_all = {}

    def push(h, m, bit, value):
        xs[h, m] = value.astype(bf16)
        x_all[h, m] = send(
            xs.at[h, m], xr.at[h, m], x_s.at[h, m], x_r.at[h, m], {"gc": flip(g, bit)}
        )

    def grad_rows(m):
        at = pl.ds(pl.multiple_of(flip(g, m) * depth, depth), depth)
        ac[m] = jnp.dot(ft[at, :], back, preferred_element_type=f32)

    def gathered(h, m):
        total = ac[m, :, h * part:(h + 1) * part]
        for bit in sides[h]:
            if m & bit:
                break
            x_all[h, m + bit].wait_recv()
            total = total + xr[h, m + bit].astype(f32)
        return total

    def rank(h, m):
        return sum(1 << t for t, bit in enumerate(sides[h]) if m & bit)

    firsts = [order[0] for order in sides]
    for m in range(n_gc - 1, 0, -1):
        if any(m & bit for bit in firsts):
            grad_rows(m)
            for h, bit in enumerate(firsts):
                if m & bit:
                    push(h, m, bit, ac[m, :, h * part:(h + 1) * part])
    k_all = [
        send(bq.at[peer(j)], br.at[:, cols(r)], k_s.at[j], k_r.at[j], {"gr": peer(j)})
        for j in range(1, n_gr)
    ]
    o_all = [
        send(ob.at[peer(j)], out_o.at[:, cols(r)], o_s.at[j], o_r.at[j], {"gr": peer(j)})
        for j in range(1, n_gr)
    ]
    own_o = pltpu.make_async_copy(ob.at[r], out_o.at[:, cols(r)], loc.at[5])
    own_o.start()
    br[:, cols(r)] = bq[r]
    for m in range(n_gc - 1, -1, -1):
        if not any(m & bit for bit in firsts):
            grad_rows(m)
    later = [
        sorted((m for m in range(1, n_gc) if not m & firsts[h]), key=lambda m: -rank(h, m))
        for h in range(2)
    ]
    for pair in zip(*later):
        for h, m in enumerate(pair):
            bit = next(bit for bit in sides[h] if m & bit)
            push(h, m, bit, gathered(h, m))
    for copy in k_all:
        copy.wait_recv()
    local_all.wait()
    step = 256

    def input_rows(i):
        iv[:, i * step:(i + 1) * step] = lax.dot_general(
            br[...], wv[i * step:(i + 1) * step, :], (((1,), (1,)), ((), ())),
            preferred_element_type=f32,
        )
    steps = width // step
    for i in range(steps // 2):
        input_rows(i)
    for h in range(2):
        wa[r, :, h * part:(h + 1) * part] = (gathered(h, 0) * scale).astype(bf16)
    w_far = [send(wa.at[r], wa.at[r], w_s.at[d], w_r.at[d], {"gr": ahead(d)}) for d in far]
    w_mate = send(wa.at[r], wa.at[r], w_s.at[0], w_r.at[0], {"gr": mate})
    w_out = []

    def keep(s, j):
        w_out.append(pltpu.make_async_copy(wa.at[s], wg_o.at[:, cols(s)], loc.at[7 + j]))
        w_out[-1].start()

    keep(r, 0)
    for i in range(steps // 2, steps):
        input_rows(i)
    own_i = pltpu.make_async_copy(iv, ig_o, loc.at[6])
    own_i.start()
    w_next = []
    for d in far:
        w_far[d - 1].wait_recv()
        s = behind(d)
        w_next.append(send(wa.at[s], wa.at[s], v_s.at[d], v_r.at[d], {"gr": mate}))
        keep(s, 2 * d)
    w_mate.wait_recv()
    keep(mate, 1)
    for d in far:
        w_next[d - 1].wait_recv()
        keep(behind(d) + 1 - 2 * core, 2 * d + 1)
    for copy in [f_mate, a_mate, w_mate] + a_far + a_next + w_far + w_next + c_all + k_all:
        copy.wait_send()
    for group in (f_far, f_next, x_all):
        for copy in group.values():
            copy.wait_send()
    for copy in o_all:
        copy.wait()
    for copy in w_out:
        copy.wait()
    own_o.wait()
    own_i.wait()


def finish_kernel(out_b, ig, wg_b, out_o, ig_o, wg_o, ov, iv, wv, of, wf, sem):
    loads = [
        pltpu.make_async_copy(src, dst, sem.at[i])
        for i, (src, dst) in enumerate(((ig, iv), (out_b, ov), (wg_b, wv)))
    ]
    stores = [
        pltpu.make_async_copy(src, dst, sem.at[3 + i])
        for i, (src, dst) in enumerate(((iv, ig_o), (of, out_o), (wf, wg_o)))
    ]
    for copy in loads:
        copy.start()
    loads[0].wait()
    stores[0].start()
    loads[1].wait()
    of[...] = ov[...].astype(jnp.float32)
    stores[1].start()
    loads[2].wait()
    wf[...] = wv[...].astype(jnp.float32)
    stores[2].start()
    for copy in stores:
        copy.wait()


def by_columns(features, weight, cotangent, block_values, block_codes, block_count):
    n_gr, n_gc = lax.axis_size("gr"), lax.axis_size("gc")
    rows, width = features.shape
    slots = block_values.shape[1]
    share, depth = width // n_gr, width // n_gc
    f32, bf16 = jnp.float32, jnp.bfloat16
    dma = pltpu.SemaphoreType.DMA
    everywhere = pl.BlockSpec(memory_space=pl.ANY)
    outside = pl.BlockSpec(memory_space=pltpu.HBM)
    scalars = pl.BlockSpec(memory_space=pltpu.SMEM)
    chips = n_gr // 2
    out, input_grad, weight_grad = pl.pallas_call(
        functools.partial(layer_kernel, n_gr, n_gc, (rows * n_gr * n_gc) ** (-0.5)),
        out_shape=(
            jax.ShapeDtypeStruct((rows, width), bf16),
            jax.ShapeDtypeStruct((rows, width), f32),
            jax.ShapeDtypeStruct((depth, width), bf16),
        ),
        in_specs=[outside] * 4 + [scalars] * 2,
        out_specs=(everywhere,) * 3,
        scratch_shapes=[
            pltpu.VMEM((n_gr, rows, width), bf16),
            pltpu.VMEM((width, n_gr * rows), bf16),
            pltpu.VMEM((width, share), bf16),
            pltpu.VMEM((width, width), bf16),
            pltpu.VMEM((slots, rows, rows), bf16),
            pltpu.VMEM((n_gr * rows, n_gr * rows), bf16),
            pltpu.VMEM((n_gr * rows, share), bf16),
            pltpu.VMEM((n_gr, rows, share), bf16),
            pltpu.VMEM((n_gr, rows, share), f32),
            pltpu.VMEM((n_gr, rows, share), bf16),
            pltpu.VMEM((n_gr, rows, share), bf16),
            pltpu.VMEM((rows, width), bf16),
            pltpu.VMEM((rows, width), f32),
            pltpu.VMEM((2, n_gc, depth, share // 2), bf16),
            pltpu.VMEM((2, n_gc, depth, share // 2), bf16),
            pltpu.VMEM((n_gc, depth, share), f32),
            pltpu.VMEM((n_gr, depth, share), bf16),
            dma((7 + n_gr,)),
        ]
        + [dma((chips, 2))] * 4
        + [dma((chips,))] * 8
        + [dma((n_gr,))] * 6
        + [dma((2, n_gc))] * 2,
        compiler_params=pltpu.CompilerParams(
            collective_id=0, has_side_effects=True, vmem_limit_bytes=GRANT
        ),
        cost_estimate=pl.CostEstimate(
            flops=2 * rows * width * (3 * width + 2 * n_gr * rows),
            bytes_accessed=6 * width * width,
            transcendentals=rows * width,
        ),
    )(features, weight, cotangent, block_values, block_codes, block_count)
    return pl.pallas_call(
        finish_kernel,
        out_shape=(
            jax.ShapeDtypeStruct((rows, width), f32),
            jax.ShapeDtypeStruct((rows, width), f32),
            jax.ShapeDtypeStruct((depth, width), f32),
        ),
        in_specs=[everywhere] * 3,
        out_specs=(everywhere,) * 3,
        scratch_shapes=[
            pltpu.VMEM((rows, width), bf16),
            pltpu.VMEM((rows, width), f32),
            pltpu.VMEM((depth, width), bf16),
            pltpu.VMEM((rows, width), f32),
            pltpu.VMEM((depth, width), f32),
            dma((6,)),
        ],
        compiler_params=pltpu.CompilerParams(vmem_limit_bytes=GRANT),
    )(out, input_grad, weight_grad)


def local(features, weight, cotangent, block_values, block_codes, block_count):
    n_gr, n_gc = lax.axis_size("gr"), lax.axis_size("gc")
    rows, width = features.shape
    whole = width % (256 * n_gr) == 0 and width % (16 * n_gc) == 0
    even = n_gr % 2 == 0 and n_gc in (4, 8, 16, 32)
    take = by_columns if whole and even and rows == block_values.shape[-1] else by_rows
    return take(features, weight, cotangent, block_values, block_codes, block_count)


def solution(mesh):
    in_specs = (
        P(("gr", "gc"), None),
        P(),
        P(("gr", "gc"), None),
        P(("gr", "gc"), None, None, None),
        P(("gr", "gc"), None),
        P(("gr", "gc")),
    )
    out_specs = (P(("gr", "gc"), None), P(("gr", "gc"), None), P("gc", None))
    return jax.shard_map(local, mesh=mesh, in_specs=in_specs, out_specs=out_specs, check_vma=False)
```

```python
import functools

import jax
import jax.numpy as jnp
from jax import lax
from jax.experimental import pallas as pl
from jax.experimental.pallas import tpu as pltpu
from jax.sharding import PartitionSpec as P

MESH = pl.DeviceIdType.MESH
GRANT = 62 * 1024 * 1024


def dense_tile(row_index, block_index, active, values, piece_blocks, row_blocks):
    block_size = values.shape[-1]
    select_col = (block_index[:, None] == jnp.arange(piece_blocks)[None, :]) & active[:, None]
    select_row = row_index[:, None] == jnp.arange(row_blocks)[None, :]
    tiled = jnp.einsum(
        "ka,km,kij->aimj",
        select_row.astype(jnp.bfloat16),
        select_col.astype(jnp.bfloat16),
        values,
        preferred_element_type=jnp.float32,
    )
    return tiled.astype(jnp.bfloat16).reshape(row_blocks * block_size, piece_blocks * block_size)


def aggregate(source, layout):
    row_index, block_index, active, values = layout
    node_rows = source.shape[0]
    block_size = values.shape[-1]
    row_blocks = node_rows // block_size
    portion = lax.all_gather(source, "gr", axis=0, tiled=True)
    tile = dense_tile(
        row_index, block_index, active, values, portion.shape[0] // block_size, row_blocks
    )
    return jnp.dot(tile, portion, preferred_element_type=jnp.float32)


def by_rows(features, weight, cotangent, block_values, block_codes, block_count):
    node_rows = features.shape[0]
    block_size = block_values.shape[-1]
    row_blocks = node_rows // block_size
    grid_cols = lax.axis_size("gc")
    grid_rows = lax.axis_size("gr")
    all_blocks = row_blocks * grid_rows * grid_cols
    slot_codes = block_codes[0]
    row_index = slot_codes // all_blocks
    column_block = slot_codes % all_blocks
    block_index = column_block // row_blocks // grid_cols * row_blocks + column_block % row_blocks
    active = jnp.arange(slot_codes.shape[0]) < block_count[0]
    layout = (row_index, block_index, active, block_values[0])
    projected = jnp.dot(features, weight, preferred_element_type=jnp.float32).astype(jnp.bfloat16)
    summed = aggregate(projected, layout)
    sigmoid = jax.nn.sigmoid(summed)
    output = summed * sigmoid
    act_slope = (cotangent.astype(jnp.float32) * sigmoid * (1.0 + summed * (1.0 - sigmoid))).astype(
        jnp.bfloat16
    )
    back_grad = aggregate(act_slope, layout).astype(jnp.bfloat16)
    input_grad = lax.dot_general(
        back_grad, weight, (((1,), (1,)), ((), ())), preferred_element_type=jnp.float32
    )
    grad_scale = (node_rows * grid_rows * grid_cols) ** (-0.5)
    partial_grad = (
        lax.dot_general(
            features, back_grad, (((0,), (0,)), ((), ())), preferred_element_type=jnp.float32
        )
        * grad_scale
    )
    row_share = lax.psum_scatter(partial_grad, "gc", scatter_dimension=0, tiled=True)
    weight_grad = lax.psum(row_share, "gr")
    return (output, input_grad, weight_grad)


def layer_kernel(
    n_gr, n_gc, scale,
    feat, wt, cot, vals, codes, count,
    out_o, ig_o, wg_o,
    fa, ft, wq, wv, vv, aa, pj, cq, sl, ob, px, oe, bq, br, iv, xs, xr, ac, wa,
    loc, f_s, f_r, g_s, g_r, a_s, a_r, b_s, b_r, w_s, w_r, v_s, v_r,
    c_s, c_r, o_s, o_r, k_s, k_r, x_s, x_r,
):
    rows, width = feat.shape
    share = width // n_gr
    chips = n_gr // 2
    r, g = lax.axis_index("gr"), lax.axis_index("gc")
    chip, core = r // 2, r % 2
    mate = chip * 2 + 1 - core
    f32, bf16 = jnp.float32, jnp.bfloat16

    def rowsof(s):
        return pl.ds(pl.multiple_of(s * rows, rows), rows)

    def cols(s):
        return pl.ds(pl.multiple_of(s * share, share), share)

    def flip(at, m):
        for bit in (1 << b for b in range(n_gc.bit_length())):
            if m & bit:
                at = at + bit - 2 * bit * (at // bit % 2)
        return at

    def send(src, dst, ss, rs, where):
        copy = pltpu.make_async_remote_copy(
            src_ref=src, dst_ref=dst, send_sem=ss, recv_sem=rs, device_id=where,
            device_id_type=MESH,
        )
        copy.start()
        return copy

    def peer(j):
        return lax.rem(r + j, n_gr)

    local_w = pltpu.make_async_copy(wt.at[:, cols(r)], wq, loc.at[0])
    local_f = pltpu.make_async_copy(feat, fa.at[r], loc.at[1])
    local_v = pltpu.make_async_copy(vals.at[0], vv, loc.at[2])
    local_c = pltpu.make_async_copy(cot.at[:, cols(r)], cq.at[r], loc.at[3])
    local_all = pltpu.make_async_copy(wt, wv, loc.at[4])
    for copy in (local_v, local_f, local_w, local_c, local_all):
        copy.start()

    barrier = pltpu.get_barrier_semaphore()
    for j in range(1, n_gr):
        pl.semaphore_signal(barrier, inc=1, device_id={"gr": peer(j)}, device_id_type=MESH)
    bits = [1 << b for b in range(n_gc.bit_length() - 1)]
    for bit in bits:
        pl.semaphore_signal(barrier, inc=1, device_id={"gc": flip(g, bit)}, device_id_type=MESH)
    pl.semaphore_wait(barrier, n_gr - 1 + len(bits))

    far = range(1, chips)
    half = rows // 2
    halves = (pl.ds(0, half), pl.ds(half, half))

    def ahead(d):
        return lax.rem(chip + d, chips) * 2 + core

    def behind(d):
        return lax.rem(chip + chips - d, chips) * 2 + core

    f_far = {
        (d, h): send(
            feat.at[part, :], fa.at[r, part, :], f_s.at[d, h], f_r.at[d, h], {"gr": ahead(d)}
        )
        for h, part in enumerate(halves)
        for d in far
    }
    f_mate = send(feat, fa.at[r], f_s.at[0, 0], f_r.at[0, 0], {"gr": mate})

    local_v.wait()
    for m in range(n_gr):
        tile = jnp.zeros((rows, rows), f32)
        for k in range(vv.shape[0]):
            hit = jnp.logical_and(k < count[0], (codes[0, k] % (n_gr * n_gc)) // n_gc == m)
            tile = tile + vv[k].astype(f32) * jnp.where(hit, 1.0, 0.0)
        aa[rowsof(r), m * rows:(m + 1) * rows] = tile.astype(bf16)

    def listed(s):
        if chips == 2:
            pair = pl.ds(pl.multiple_of(s // 2 * (2 * rows), 2 * rows), 2 * rows)
            return aa.at[rowsof(s), pair]
        return aa.at[rowsof(s), :]

    a_far = [send(listed(r), listed(r), a_s.at[d], a_r.at[d], {"gr": ahead(d)}) for d in far]
    a_mate = send(aa.at[rowsof(r)], aa.at[rowsof(r)], a_s.at[0], a_r.at[0], {"gr": mate})

    def project(s):
        pj[rowsof(s), :] = jnp.dot(fa[s], wq[...], preferred_element_type=f32).astype(bf16)

    def turn(s):
        ft[:, rowsof(s)] = fa[s].T

    local_f.wait()
    local_w.wait()
    project(r)
    turn(r)
    f_mate.wait_recv()
    project(mate)
    turn(mate)

    f_next = {}
    c_all = []
    for h, part in enumerate(halves):
        for d in far:
            f_far[d, h].wait_recv()
            here = fa.at[behind(d), part, :]
            f_next[d, h] = send(here, here, g_s.at[d, h], g_r.at[d, h], {"gr": mate})
        if h == 0:
            c_all = [
                send(cot.at[:, cols(peer(j))], cq.at[r], c_s.at[j], c_r.at[j], {"gr": peer(j)})
                for j in range(1, n_gr)
            ]
    a_next = []
    for d in far:
        a_far[d - 1].wait_recv()
        here = listed(behind(d))
        a_next.append(send(here, here, b_s.at[d], b_r.at[d], {"gr": mate}))
    for d in far:
        project(behind(d))
    a_mate.wait_recv()
    if chips == 2:
        for t in (r, mate):
            for s in (lax.rem(chip + 1, 2) * 2, lax.rem(chip + 1, 2) * 2 + 1):
                aa[rowsof(s), rowsof(t)] = aa[rowsof(t), rowsof(s)].T
    for d in far:
        for h in range(2):
            f_next[d, h].wait_recv()
        project(behind(d) + 1 - 2 * core)
    for copy in a_next:
        copy.wait_recv()

    for i in range(n_gr):
        summed = jnp.dot(aa[i * rows:(i + 1) * rows, :], pj[...], preferred_element_type=f32)
        sigmoid = jax.nn.sigmoid(summed)
        ob[i] = summed * sigmoid
        sl[i] = sigmoid * (1.0 + summed * (1.0 - sigmoid))
    for d in far:
        turn(behind(d))
        turn(behind(d) + 1 - 2 * core)
    local_c.wait()
    for copy in c_all:
        copy.wait_recv()
    slope_all = (cq[...].astype(f32) * sl[...]).astype(bf16).reshape(n_gr * rows, share)
    for i in range(n_gr):
        bq[i] = jnp.dot(
            aa[i * rows:(i + 1) * rows, :], slope_all, preferred_element_type=f32
        ).astype(bf16)
    back = bq[...].reshape(n_gr * rows, share)

    depth, part = width // n_gc, share // 2
    sides = [bits, bits[1::-1] + bits[2:]]
    x_all = {}

    def push(h, m, bit, value):
        xs[h, m] = value.astype(bf16)
        x_all[h, m] = send(
            xs.at[h, m], xr.at[h, m], x_s.at[h, m], x_r.at[h, m], {"gc": flip(g, bit)}
        )

    def grad_rows(m):
        at = pl.ds(pl.multiple_of(flip(g, m) * depth, depth), depth)
        ac[m] = jnp.dot(ft[at, :], back, preferred_element_type=f32)

    def gathered(h, m):
        total = ac[m, :, h * part:(h + 1) * part]
        for bit in sides[h]:
            if m & bit:
                break
            x_all[h, m + bit].wait_recv()
            total = total + xr[h, m + bit].astype(f32)
        return total

    def rank(h, m):
        return sum(1 << t for t, bit in enumerate(sides[h]) if m & bit)

    firsts = [order[0] for order in sides]
    for m in range(n_gc - 1, 0, -1):
        if any(m & bit for bit in firsts):
            grad_rows(m)
            for h, bit in enumerate(firsts):
                if m & bit:
                    push(h, m, bit, ac[m, :, h * part:(h + 1) * part])
    k_all = [
        send(bq.at[peer(j)], br.at[:, cols(r)], k_s.at[j], k_r.at[j], {"gr": peer(j)})
        for j in range(1, n_gr)
    ]
    o_all = [send(ob.at[mate], out_o.at[:, cols(r)], o_s.at[0], o_r.at[0], {"gr": mate})]
    o_own = [pltpu.make_async_copy(ob.at[r], out_o.at[:, cols(r)], loc.at[5])]
    o_own[0].start()
    br[:, cols(r)] = bq[r]
    for m in range(n_gc - 1, -1, -1):
        if not any(m & bit for bit in firsts):
            grad_rows(m)
    later = [
        sorted((m for m in range(1, n_gc) if not m & firsts[h]), key=lambda m: -rank(h, m))
        for h in range(2)
    ]

    def other_outputs():
        local_all.wait()
        for d in far:
            q = behind(d)
            px[...] = jnp.dot(
                fa[...].reshape(n_gr * rows, width), wv[:, cols(q)], preferred_element_type=f32
            ).astype(bf16)
            for side, s in enumerate((mate, r)):
                summed = jnp.dot(aa[rowsof(s), :], px[...], preferred_element_type=f32)
                oe[d, side] = summed * jax.nn.sigmoid(summed)
            o_all.append(
                send(oe.at[d, 0], out_o.at[:, cols(q)], o_s.at[d], o_r.at[d], {"gr": mate})
            )
            o_own.append(
                pltpu.make_async_copy(oe.at[d, 1], out_o.at[:, cols(q)], loc.at[6 + n_gr + d])
            )
            o_own[-1].start()

    for turn_of, pair in enumerate(zip(*later)):
        if turn_of == 1:
            other_outputs()
        for h, m in enumerate(pair):
            bit = next(bit for bit in sides[h] if m & bit)
            push(h, m, bit, gathered(h, m))
    if len(later[0]) < 2:
        other_outputs()
    for copy in k_all:
        copy.wait_recv()
    step = 256

    def input_rows(i):
        iv[:, i * step:(i + 1) * step] = lax.dot_general(
            br[...], wv[i * step:(i + 1) * step, :], (((1,), (1,)), ((), ())),
            preferred_element_type=f32,
        )
    steps = width // step
    for i in range(steps // 2):
        input_rows(i)
    for h in range(2):
        wa[r, :, h * part:(h + 1) * part] = (gathered(h, 0) * scale).astype(bf16)
    w_far = [send(wa.at[r], wa.at[r], w_s.at[d], w_r.at[d], {"gr": ahead(d)}) for d in far]
    w_mate = send(wa.at[r], wa.at[r], w_s.at[0], w_r.at[0], {"gr": mate})
    w_out = []

    def keep(s, j):
        w_out.append(pltpu.make_async_copy(wa.at[s], wg_o.at[:, cols(s)], loc.at[7 + j]))
        w_out[-1].start()

    keep(r, 0)
    for i in range(steps // 2, steps):
        input_rows(i)
    own_i = pltpu.make_async_copy(iv, ig_o, loc.at[6])
    own_i.start()
    w_next = []
    for d in far:
        w_far[d - 1].wait_recv()
        s = behind(d)
        w_next.append(send(wa.at[s], wa.at[s], v_s.at[d], v_r.at[d], {"gr": mate}))
        keep(s, 2 * d)
    w_mate.wait_recv()
    keep(mate, 1)
    for d in far:
        w_next[d - 1].wait_recv()
        keep(behind(d) + 1 - 2 * core, 2 * d + 1)
    for copy in [f_mate, a_mate, w_mate] + a_far + a_next + w_far + w_next + c_all + k_all:
        copy.wait_send()
    for group in (f_far, f_next, x_all):
        for copy in group.values():
            copy.wait_send()
    for copy in o_all:
        copy.wait()
    for copy in w_out:
        copy.wait()
    for copy in o_own:
        copy.wait()
    own_i.wait()


def finish_kernel(out_b, ig, wg_b, out_o, ig_o, wg_o, ov, iv, wv, wf, sem):
    loads = [
        pltpu.make_async_copy(src, dst, sem.at[i])
        for i, (src, dst) in enumerate(((ig, iv), (out_b, ov), (wg_b, wv)))
    ]
    stores = [
        pltpu.make_async_copy(src, dst, sem.at[3 + i])
        for i, (src, dst) in enumerate(((iv, ig_o), (ov, out_o), (wf, wg_o)))
    ]
    for copy in loads:
        copy.start()
    loads[0].wait()
    stores[0].start()
    loads[1].wait()
    stores[1].start()
    loads[2].wait()
    wf[...] = wv[...].astype(jnp.float32)
    stores[2].start()
    for copy in stores:
        copy.wait()


def by_columns(features, weight, cotangent, block_values, block_codes, block_count):
    n_gr, n_gc = lax.axis_size("gr"), lax.axis_size("gc")
    rows, width = features.shape
    slots = block_values.shape[1]
    share, depth = width // n_gr, width // n_gc
    f32, bf16 = jnp.float32, jnp.bfloat16
    dma = pltpu.SemaphoreType.DMA
    everywhere = pl.BlockSpec(memory_space=pl.ANY)
    outside = pl.BlockSpec(memory_space=pltpu.HBM)
    scalars = pl.BlockSpec(memory_space=pltpu.SMEM)
    chips = n_gr // 2
    out, input_grad, weight_grad = pl.pallas_call(
        functools.partial(layer_kernel, n_gr, n_gc, (rows * n_gr * n_gc) ** (-0.5)),
        out_shape=(
            jax.ShapeDtypeStruct((rows, width), f32),
            jax.ShapeDtypeStruct((rows, width), f32),
            jax.ShapeDtypeStruct((depth, width), bf16),
        ),
        in_specs=[outside] * 4 + [scalars] * 2,
        out_specs=(everywhere,) * 3,
        scratch_shapes=[
            pltpu.VMEM((n_gr, rows, width), bf16),
            pltpu.VMEM((width, n_gr * rows), bf16),
            pltpu.VMEM((width, share), bf16),
            pltpu.VMEM((width, width), bf16),
            pltpu.VMEM((slots, rows, rows), bf16),
            pltpu.VMEM((n_gr * rows, n_gr * rows), bf16),
            pltpu.VMEM((n_gr * rows, share), bf16),
            pltpu.VMEM((n_gr, rows, share), bf16),
            pltpu.VMEM((n_gr, rows, share), f32),
            pltpu.VMEM((n_gr, rows, share), f32),
            pltpu.VMEM((n_gr * rows, share), bf16),
            pltpu.VMEM((chips, 2, rows, share), f32),
            pltpu.VMEM((n_gr, rows, share), bf16),
            pltpu.VMEM((rows, width), bf16),
            pltpu.VMEM((rows, width), f32),
            pltpu.VMEM((2, n_gc, depth, share // 2), bf16),
            pltpu.VMEM((2, n_gc, depth, share // 2), bf16),
            pltpu.VMEM((n_gc, depth, share), f32),
            pltpu.VMEM((n_gr, depth, share), bf16),
            dma((6 + n_gr + chips,)),
        ]
        + [dma((chips, 2))] * 4
        + [dma((chips,))] * 8
        + [dma((n_gr,))] * 6
        + [dma((2, n_gc))] * 2,
        compiler_params=pltpu.CompilerParams(
            collective_id=0, has_side_effects=True, vmem_limit_bytes=GRANT
        ),
        cost_estimate=pl.CostEstimate(
            flops=2 * rows * width * (3 * width + 2 * n_gr * rows),
            bytes_accessed=6 * width * width,
            transcendentals=rows * width,
        ),
    )(features, weight, cotangent, block_values, block_codes, block_count)
    return pl.pallas_call(
        finish_kernel,
        out_shape=(
            jax.ShapeDtypeStruct((rows, width), f32),
            jax.ShapeDtypeStruct((rows, width), f32),
            jax.ShapeDtypeStruct((depth, width), f32),
        ),
        in_specs=[everywhere] * 3,
        out_specs=(everywhere,) * 3,
        scratch_shapes=[
            pltpu.VMEM((rows, width), f32),
            pltpu.VMEM((rows, width), f32),
            pltpu.VMEM((depth, width), bf16),
            pltpu.VMEM((depth, width), f32),
            dma((6,)),
        ],
        compiler_params=pltpu.CompilerParams(vmem_limit_bytes=GRANT),
    )(out, input_grad, weight_grad)


def local(features, weight, cotangent, block_values, block_codes, block_count):
    n_gr, n_gc = lax.axis_size("gr"), lax.axis_size("gc")
    rows, width = features.shape
    whole = width % (256 * n_gr) == 0 and width % (16 * n_gc) == 0
    even = n_gr % 2 == 0 and n_gc in (4, 8, 16, 32)
    take = by_columns if whole and even and rows == block_values.shape[-1] else by_rows
    return take(features, weight, cotangent, block_values, block_codes, block_count)


def solution(mesh):
    in_specs = (
        P(("gr", "gc"), None),
        P(),
        P(("gr", "gc"), None),
        P(("gr", "gc"), None, None, None),
        P(("gr", "gc"), None),
        P(("gr", "gc")),
    )
    out_specs = (P(("gr", "gc"), None), P(("gr", "gc"), None), P("gc", None))
    return jax.shard_map(local, mesh=mesh, in_specs=in_specs, out_specs=out_specs, check_vma=False)
```

```python
import functools

import jax
import jax.numpy as jnp
from jax import lax
from jax.experimental import pallas as pl
from jax.experimental.pallas import tpu as pltpu
from jax.sharding import PartitionSpec as P

MESH = pl.DeviceIdType.MESH
GRANT = 62 * 1024 * 1024


def dense_tile(row_index, block_index, active, values, piece_blocks, row_blocks):
    block_size = values.shape[-1]
    select_col = (block_index[:, None] == jnp.arange(piece_blocks)[None, :]) & active[:, None]
    select_row = row_index[:, None] == jnp.arange(row_blocks)[None, :]
    tiled = jnp.einsum(
        "ka,km,kij->aimj",
        select_row.astype(jnp.bfloat16),
        select_col.astype(jnp.bfloat16),
        values,
        preferred_element_type=jnp.float32,
    )
    return tiled.astype(jnp.bfloat16).reshape(row_blocks * block_size, piece_blocks * block_size)


def aggregate(source, layout):
    row_index, block_index, active, values = layout
    node_rows = source.shape[0]
    block_size = values.shape[-1]
    row_blocks = node_rows // block_size
    portion = lax.all_gather(source, "gr", axis=0, tiled=True)
    tile = dense_tile(
        row_index, block_index, active, values, portion.shape[0] // block_size, row_blocks
    )
    return jnp.dot(tile, portion, preferred_element_type=jnp.float32)


def by_rows(features, weight, cotangent, block_values, block_codes, block_count):
    node_rows = features.shape[0]
    block_size = block_values.shape[-1]
    row_blocks = node_rows // block_size
    grid_cols = lax.axis_size("gc")
    grid_rows = lax.axis_size("gr")
    all_blocks = row_blocks * grid_rows * grid_cols
    slot_codes = block_codes[0]
    row_index = slot_codes // all_blocks
    column_block = slot_codes % all_blocks
    block_index = column_block // row_blocks // grid_cols * row_blocks + column_block % row_blocks
    active = jnp.arange(slot_codes.shape[0]) < block_count[0]
    layout = (row_index, block_index, active, block_values[0])
    projected = jnp.dot(features, weight, preferred_element_type=jnp.float32).astype(jnp.bfloat16)
    summed = aggregate(projected, layout)
    sigmoid = jax.nn.sigmoid(summed)
    output = summed * sigmoid
    act_slope = (cotangent.astype(jnp.float32) * sigmoid * (1.0 + summed * (1.0 - sigmoid))).astype(
        jnp.bfloat16
    )
    back_grad = aggregate(act_slope, layout).astype(jnp.bfloat16)
    input_grad = lax.dot_general(
        back_grad, weight, (((1,), (1,)), ((), ())), preferred_element_type=jnp.float32
    )
    grad_scale = (node_rows * grid_rows * grid_cols) ** (-0.5)
    partial_grad = (
        lax.dot_general(
            features, back_grad, (((0,), (0,)), ((), ())), preferred_element_type=jnp.float32
        )
        * grad_scale
    )
    row_share = lax.psum_scatter(partial_grad, "gc", scatter_dimension=0, tiled=True)
    weight_grad = lax.psum(row_share, "gr")
    return (output, input_grad, weight_grad)


def layer_kernel(
    n_gr, n_gc, scale,
    feat, wt, cot, vals, codes, count,
    out_o, ig_o, wg_o,
    fa, ft, wq, wv, vv, aa, pj, cq, sl, ob, px, oe, bq, br, iv, xs, xr, ac, wa,
    loc, f_s, f_r, g_s, g_r, a_s, a_r, b_s, b_r, w_s, w_r, v_s, v_r,
    c_s, c_r, o_s, o_r, k_s, k_r, x_s, x_r,
):
    rows, width = feat.shape
    share = width // n_gr
    chips = n_gr // 2
    r, g = lax.axis_index("gr"), lax.axis_index("gc")
    chip, core = r // 2, r % 2
    mate = chip * 2 + 1 - core
    f32, bf16 = jnp.float32, jnp.bfloat16

    def rowsof(s):
        return pl.ds(pl.multiple_of(s * rows, rows), rows)

    def cols(s):
        return pl.ds(pl.multiple_of(s * share, share), share)

    def flip(at, m):
        for bit in (1 << b for b in range(n_gc.bit_length())):
            if m & bit:
                at = at + bit - 2 * bit * (at // bit % 2)
        return at

    def send(src, dst, ss, rs, where):
        copy = pltpu.make_async_remote_copy(
            src_ref=src, dst_ref=dst, send_sem=ss, recv_sem=rs, device_id=where,
            device_id_type=MESH,
        )
        copy.start()
        return copy

    def peer(j):
        return lax.rem(r + j, n_gr)

    local_w = pltpu.make_async_copy(wt.at[:, cols(r)], wq, loc.at[0])
    local_f = pltpu.make_async_copy(feat, fa.at[r], loc.at[1])
    local_v = pltpu.make_async_copy(vals.at[0], vv, loc.at[2])
    local_c = pltpu.make_async_copy(cot.at[:, cols(r)], cq.at[r], loc.at[3])
    local_all = pltpu.make_async_copy(wt, wv, loc.at[4])
    for copy in (local_v, local_f, local_w, local_c, local_all):
        copy.start()

    barrier = pltpu.get_barrier_semaphore()
    for j in range(1, n_gr):
        pl.semaphore_signal(barrier, inc=1, device_id={"gr": peer(j)}, device_id_type=MESH)
    bits = [1 << b for b in range(n_gc.bit_length() - 1)]
    for bit in bits:
        pl.semaphore_signal(barrier, inc=1, device_id={"gc": flip(g, bit)}, device_id_type=MESH)
    pl.semaphore_wait(barrier, n_gr - 1 + len(bits))

    far = range(1, chips)
    half = rows // 2
    halves = (pl.ds(0, half), pl.ds(half, half))

    def ahead(d):
        return lax.rem(chip + d, chips) * 2 + core

    def behind(d):
        return lax.rem(chip + chips - d, chips) * 2 + core

    f_far = {
        (d, h): send(
            feat.at[part, :], fa.at[r, part, :], f_s.at[d, h], f_r.at[d, h], {"gr": ahead(d)}
        )
        for h, part in enumerate(halves)
        for d in far
    }
    f_mate = send(feat, fa.at[r], f_s.at[0, 0], f_r.at[0, 0], {"gr": mate})

    local_v.wait()
    for m in range(n_gr):
        tile = jnp.zeros((rows, rows), f32)
        for k in range(vv.shape[0]):
            hit = jnp.logical_and(k < count[0], (codes[0, k] % (n_gr * n_gc)) // n_gc == m)
            tile = tile + vv[k].astype(f32) * jnp.where(hit, 1.0, 0.0)
        aa[rowsof(r), m * rows:(m + 1) * rows] = tile.astype(bf16)

    def listed(s):
        if chips == 2:
            pair = pl.ds(pl.multiple_of(s // 2 * (2 * rows), 2 * rows), 2 * rows)
            return aa.at[rowsof(s), pair]
        return aa.at[rowsof(s), :]

    a_far = [send(listed(r), listed(r), a_s.at[d], a_r.at[d], {"gr": ahead(d)}) for d in far]
    a_mate = send(aa.at[rowsof(r)], aa.at[rowsof(r)], a_s.at[0], a_r.at[0], {"gr": mate})

    def project(s):
        pj[rowsof(s), :] = jnp.dot(fa[s], wq[...], preferred_element_type=f32).astype(bf16)

    def project_other(d, c):
        at = pl.ds(pl.multiple_of(c * 2 * rows, 2 * rows), 2 * rows)
        px[d, at, :] = jnp.dot(
            fa[pl.ds(c * 2, 2)].reshape(2 * rows, width), wv[:, cols(behind(d))],
            preferred_element_type=f32,
        ).astype(bf16)

    def turn(s):
        ft[:, rowsof(s)] = fa[s].T

    local_f.wait()
    local_w.wait()
    project(r)
    turn(r)
    f_mate.wait_recv()
    project(mate)
    turn(mate)
    local_all.wait()
    for d in far:
        project_other(d, chip)

    f_next = {}
    c_all = []
    for h, part in enumerate(halves):
        for d in far:
            f_far[d, h].wait_recv()
            here = fa.at[behind(d), part, :]
            f_next[d, h] = send(here, here, g_s.at[d, h], g_r.at[d, h], {"gr": mate})
        if h == 0:
            c_all = [
                send(cot.at[:, cols(peer(j))], cq.at[r], c_s.at[j], c_r.at[j], {"gr": peer(j)})
                for j in range(1, n_gr)
            ]
    a_next = []
    for d in far:
        a_far[d - 1].wait_recv()
        here = listed(behind(d))
        a_next.append(send(here, here, b_s.at[d], b_r.at[d], {"gr": mate}))
    for d in far:
        project(behind(d))
    a_mate.wait_recv()
    if chips == 2:
        for t in (r, mate):
            for s in (lax.rem(chip + 1, 2) * 2, lax.rem(chip + 1, 2) * 2 + 1):
                aa[rowsof(s), rowsof(t)] = aa[rowsof(t), rowsof(s)].T
    for d in far:
        for h in range(2):
            f_next[d, h].wait_recv()
        project(behind(d) + 1 - 2 * core)
    for copy in a_next:
        copy.wait_recv()

    sl[...] = jnp.dot(aa[...], pj[...], preferred_element_type=f32).reshape(sl.shape)
    for i in range(n_gr):
        summed = sl[i]
        sigmoid = jax.nn.sigmoid(summed)
        ob[i] = summed * sigmoid
        sl[i] = sigmoid * (1.0 + summed * (1.0 - sigmoid))
    for d in far:
        turn(behind(d))
        turn(behind(d) + 1 - 2 * core)
    local_c.wait()
    for copy in c_all:
        copy.wait_recv()
    slope_all = (cq[...].astype(f32) * sl[...]).astype(bf16).reshape(n_gr * rows, share)
    back = jnp.dot(aa[...], slope_all, preferred_element_type=f32).astype(bf16)
    bq[...] = back.reshape(bq.shape)

    depth, part = width // n_gc, share // 2
    sides = [bits, bits[1::-1] + bits[2:]]
    x_all = {}

    def push(h, m, bit, value):
        xs[h, m] = value.astype(bf16)
        x_all[h, m] = send(
            xs.at[h, m], xr.at[h, m], x_s.at[h, m], x_r.at[h, m], {"gc": flip(g, bit)}
        )

    def grad_rows(top):
        at = flip(g, top) // bits[-1] * bits[-1] * depth
        at = pl.ds(pl.multiple_of(at, bits[-1] * depth), bits[-1] * depth)
        ac[at, :] = jnp.dot(
            ft[at, :], bq[...].reshape(n_gr * rows, share), preferred_element_type=f32
        )

    def own_part(h, m):
        at = pl.ds(pl.multiple_of(flip(g, m) * depth, depth), depth)
        return ac[at, h * part:(h + 1) * part]

    def gathered(h, m):
        total = own_part(h, m)
        for bit in sides[h]:
            if m & bit:
                break
            x_all[h, m + bit].wait_recv()
            total = total + xr[h, m + bit].astype(f32)
        return total

    def rank(h, m):
        return sum(1 << t for t, bit in enumerate(sides[h]) if m & bit)

    firsts = [order[0] for order in sides]
    for top in (bits[-1], 0):
        grad_rows(top)
        for m in range(top + bits[-1] - 1, max(top - 1, 0), -1):
            for h, bit in enumerate(firsts):
                if m & bit:
                    push(h, m, bit, own_part(h, m))
    k_all = [
        send(bq.at[peer(j)], br.at[:, cols(r)], k_s.at[j], k_r.at[j], {"gr": peer(j)})
        for j in range(1, n_gr)
    ]
    o_all = [send(ob.at[mate], out_o.at[:, cols(r)], o_s.at[0], o_r.at[0], {"gr": mate})]
    o_own = [pltpu.make_async_copy(ob.at[r], out_o.at[:, cols(r)], loc.at[5])]
    o_own[0].start()
    br[:, cols(r)] = bq[r]
    later = [
        sorted((m for m in range(1, n_gc) if not m & firsts[h]), key=lambda m: -rank(h, m))
        for h in range(2)
    ]

    def other_outputs():
        for d in far:
            q = behind(d)
            for e in far:
                project_other(d, lax.rem(chip + e, chips))
            for side, s in enumerate((mate, r)):
                summed = jnp.dot(aa[rowsof(s), :], px[d], preferred_element_type=f32)
                oe[d, side] = summed * jax.nn.sigmoid(summed)
            o_all.append(
                send(oe.at[d, 0], out_o.at[:, cols(q)], o_s.at[d], o_r.at[d], {"gr": mate})
            )
            o_own.append(
                pltpu.make_async_copy(oe.at[d, 1], out_o.at[:, cols(q)], loc.at[6 + n_gr + d])
            )
            o_own[-1].start()

    for turn_of, pair in enumerate(zip(*later)):
        if turn_of == 1:
            other_outputs()
        for h, m in enumerate(pair):
            bit = next(bit for bit in sides[h] if m & bit)
            push(h, m, bit, gathered(h, m))
    if len(later[0]) < 2:
        other_outputs()
    for copy in k_all:
        copy.wait_recv()
    step = 256

    def input_rows(i):
        iv[:, i * step:(i + 1) * step] = lax.dot_general(
            br[...], wv[i * step:(i + 1) * step, :], (((1,), (1,)), ((), ())),
            preferred_element_type=f32,
        )
    steps = width // step
    for i in range(steps // 2):
        input_rows(i)
    for h in range(2):
        wa[r, :, h * part:(h + 1) * part] = (gathered(h, 0) * scale).astype(bf16)
    w_far = [send(wa.at[r], wa.at[r], w_s.at[d], w_r.at[d], {"gr": ahead(d)}) for d in far]
    w_mate = send(wa.at[r], wa.at[r], w_s.at[0], w_r.at[0], {"gr": mate})
    w_out = []

    def keep(s, j):
        w_out.append(pltpu.make_async_copy(wa.at[s], wg_o.at[:, cols(s)], loc.at[7 + j]))
        w_out[-1].start()

    keep(r, 0)
    for i in range(steps // 2, steps):
        input_rows(i)
    own_i = pltpu.make_async_copy(iv, ig_o, loc.at[6])
    own_i.start()
    w_next = []
    for d in far:
        w_far[d - 1].wait_recv()
        s = behind(d)
        w_next.append(send(wa.at[s], wa.at[s], v_s.at[d], v_r.at[d], {"gr": mate}))
        keep(s, 2 * d)
    w_mate.wait_recv()
    keep(mate, 1)
    for d in far:
        w_next[d - 1].wait_recv()
        keep(behind(d) + 1 - 2 * core, 2 * d + 1)
    for copy in [f_mate, a_mate, w_mate] + a_far + a_next + w_far + w_next + c_all + k_all:
        copy.wait_send()
    for group in (f_far, f_next, x_all):
        for copy in group.values():
            copy.wait_send()
    for copy in o_all:
        copy.wait()
    for copy in w_out:
        copy.wait()
    for copy in o_own:
        copy.wait()
    own_i.wait()


def finish_kernel(out_b, ig, wg_b, out_o, ig_o, wg_o, ov, iv, wv, wf, sem):
    loads = [
        pltpu.make_async_copy(src, dst, sem.at[i])
        for i, (src, dst) in enumerate(((ig, iv), (out_b, ov), (wg_b, wv)))
    ]
    stores = [
        pltpu.make_async_copy(src, dst, sem.at[3 + i])
        for i, (src, dst) in enumerate(((iv, ig_o), (ov, out_o), (wf, wg_o)))
    ]
    for copy in loads:
        copy.start()
    loads[0].wait()
    stores[0].start()
    loads[1].wait()
    stores[1].start()
    loads[2].wait()
    wf[...] = wv[...].astype(jnp.float32)
    stores[2].start()
    for copy in stores:
        copy.wait()


def by_columns(features, weight, cotangent, block_values, block_codes, block_count):
    n_gr, n_gc = lax.axis_size("gr"), lax.axis_size("gc")
    rows, width = features.shape
    slots = block_values.shape[1]
    share, depth = width // n_gr, width // n_gc
    f32, bf16 = jnp.float32, jnp.bfloat16
    dma = pltpu.SemaphoreType.DMA
    everywhere = pl.BlockSpec(memory_space=pl.ANY)
    outside = pl.BlockSpec(memory_space=pltpu.HBM)
    scalars = pl.BlockSpec(memory_space=pltpu.SMEM)
    chips = n_gr // 2
    out, input_grad, weight_grad = pl.pallas_call(
        functools.partial(layer_kernel, n_gr, n_gc, (rows * n_gr * n_gc) ** (-0.5)),
        out_shape=(
            jax.ShapeDtypeStruct((rows, width), f32),
            jax.ShapeDtypeStruct((rows, width), f32),
            jax.ShapeDtypeStruct((depth, width), bf16),
        ),
        in_specs=[outside] * 4 + [scalars] * 2,
        out_specs=(everywhere,) * 3,
        scratch_shapes=[
            pltpu.VMEM((n_gr, rows, width), bf16),
            pltpu.VMEM((width, n_gr * rows), bf16),
            pltpu.VMEM((width, share), bf16),
            pltpu.VMEM((width, width), bf16),
            pltpu.VMEM((slots, rows, rows), bf16),
            pltpu.VMEM((n_gr * rows, n_gr * rows), bf16),
            pltpu.VMEM((n_gr * rows, share), bf16),
            pltpu.VMEM((n_gr, rows, share), bf16),
            pltpu.VMEM((n_gr, rows, share), f32),
            pltpu.VMEM((n_gr, rows, share), f32),
            pltpu.VMEM((chips, n_gr * rows, share), bf16),
            pltpu.VMEM((chips, 2, rows, share), f32),
            pltpu.VMEM((n_gr, rows, share), bf16),
            pltpu.VMEM((rows, width), bf16),
            pltpu.VMEM((rows, width), f32),
            pltpu.VMEM((2, n_gc, depth, share // 2), bf16),
            pltpu.VMEM((2, n_gc, depth, share // 2), bf16),
            pltpu.VMEM((n_gc * depth, share), f32),
            pltpu.VMEM((n_gr, depth, share), bf16),
            dma((6 + n_gr + chips,)),
        ]
        + [dma((chips, 2))] * 4
        + [dma((chips,))] * 8
        + [dma((n_gr,))] * 6
        + [dma((2, n_gc))] * 2,
        compiler_params=pltpu.CompilerParams(
            collective_id=0, has_side_effects=True, vmem_limit_bytes=GRANT
        ),
        cost_estimate=pl.CostEstimate(
            flops=2 * rows * width * (3 * width + 2 * n_gr * rows),
            bytes_accessed=6 * width * width,
            transcendentals=rows * width,
        ),
    )(features, weight, cotangent, block_values, block_codes, block_count)
    return pl.pallas_call(
        finish_kernel,
        out_shape=(
            jax.ShapeDtypeStruct((rows, width), f32),
            jax.ShapeDtypeStruct((rows, width), f32),
            jax.ShapeDtypeStruct((depth, width), f32),
        ),
        in_specs=[everywhere] * 3,
        out_specs=(everywhere,) * 3,
        scratch_shapes=[
            pltpu.VMEM((rows, width), f32),
            pltpu.VMEM((rows, width), f32),
            pltpu.VMEM((depth, width), bf16),
            pltpu.VMEM((depth, width), f32),
            dma((6,)),
        ],
        compiler_params=pltpu.CompilerParams(vmem_limit_bytes=GRANT),
    )(out, input_grad, weight_grad)


def local(features, weight, cotangent, block_values, block_codes, block_count):
    n_gr, n_gc = lax.axis_size("gr"), lax.axis_size("gc")
    rows, width = features.shape
    whole = width % (256 * n_gr) == 0 and width % (16 * n_gc) == 0
    even = n_gr % 2 == 0 and n_gc in (4, 8, 16, 32)
    take = by_columns if whole and even and rows == block_values.shape[-1] else by_rows
    return take(features, weight, cotangent, block_values, block_codes, block_count)


def solution(mesh):
    in_specs = (
        P(("gr", "gc"), None),
        P(),
        P(("gr", "gc"), None),
        P(("gr", "gc"), None, None, None),
        P(("gr", "gc"), None),
        P(("gr", "gc")),
    )
    out_specs = (P(("gr", "gc"), None), P(("gr", "gc"), None), P("gc", None))
    return jax.shard_map(local, mesh=mesh, in_specs=in_specs, out_specs=out_specs, check_vma=False)
```
